512 devices in a mesh: mem: 8 (over x, core), col: 64 (over z, y).
Axes of the slice: x: 4, y: 8, z: 8, core: 2. Of those that a mesh axis runs over, the one named last changes fastest.
Arguments:
- controls: bfloat16 [8, 127, 98304], P('mem', None, 'col'), may hold values from -6 to 6
- perturbations: bfloat16 [8, 127, 98304], P('mem', None, 'col'), may hold values from -6 to 6
- vertical_filter: bfloat16 [127, 127], replicated, may hold values from -4 to 4
- scales: float32 [127], replicated, may hold values from 16 to 48
- level_counts: int32 [64], replicated, may hold values from 1 to 4, 127 in all
- weight_index: int32 [8], P('mem'), may hold values from 0 to 9
- member_weights: float32 [10], replicated, may hold values from 0.1 to 0.6
Outputs:
- increment: float32 [127, 98304], P(None, 'col')
- slab_increment: float32 [256, 64, 1536], P('col', None, 'mem')
The draws below stay inside these ranges and needn't reach their ends.
Inputs may be any that keep to these rules, and one draw needn't show every extreme that they name: `level_counts`: the counts sum to 127; some tile owns exactly 4 levels.
All inputs are finite; a program needn't handle non-finite values.
Results may differ from the reference program's by a relative error of at most 0.0062.
Values may be sent and summed in bfloat16 or wider, within the bound.
A program may use at most 64 MiB of HBM per device.

```python
import math
import jax
import jax.numpy as jnp
import numpy as np
from jax import lax

LEV = 127
NLON = 1536
HALF = 24
NW = 10
TILES = 64
SLOTS = 4
ROWS = 256
LAT = 64
COLS = 98304
MEMBERS = 8


def draw_vertical_filter(key, part):
    rows = jnp.arange(LEV).astype(jnp.float32)[:, None]
    cols = jnp.arange(LEV).astype(jnp.float32)[None, :]
    envelope = jnp.exp(-0.5 * ((rows - cols) / 6.0) ** 2)
    identity = (rows == cols).astype(jnp.float32)
    noise = jnp.clip(jax.random.normal(jax.random.fold_in(key, 1), (LEV, LEV), jnp.float32), -4.0, 4.0)
    return (0.25 * envelope * noise + 0.6 * identity).astype(jnp.bfloat16)


def plant(entries, own_key, least, high):
    longest = entries.shape.index(max(entries.shape))
    spots = []
    for shift in (0, 1):
        where = [jax.random.randint(jax.random.fold_in(own_key, axis), (), 0, length) for axis, length in enumerate(entries.shape)]
        where[longest] = (where[longest] + shift) % entries.shape[longest]
        spots.append(tuple(where))
    return entries.at[spots[0]].set(least).at[spots[1]].set(high)


def levels(own_key, extent, shards, low, top_value):
    loudness, own = 1.0, jax.random.fold_in(own_key, 6)
    for dim, parts in shards:
        draws = jnp.exp(jax.random.uniform(jax.random.fold_in(own, dim), (parts,), jnp.float32, low / len(shards), top_value / len(shards)))
        loudness = loudness * jnp.repeat(draws, extent[dim] // parts).reshape([-1 if axis == dim else 1 for axis in range(len(extent))])
    return loudness


def length_profile(count, total, bound, slope):
    weights = [(1 << 20) // math.isqrt(standing ** slope) + 1 for standing in range(2, count + 1)]
    rest, given = total - bound - (count - 1), [1] * (count - 1)
    while rest > 0:
        candidates = [i for i in range(count - 1) if given[i] < bound]
        pool, remaining = sum([weights[i] for i in candidates]), rest
        for i in candidates:
            more = min(bound - given[i], max(1, remaining * weights[i] // pool), rest)
            given[i] = given[i] + more
            rest = rest - more
    return np.array([bound] + given)


def uneven(stream_key, number_of, total, reach, lean):
    if number_of == 2:
        one = jax.random.randint(stream_key, (), max(1, total - reach), min(reach, total - 1) + 1)
        return jnp.stack([one, total - one])
    sizes = jnp.asarray(length_profile(number_of, total, reach, lean), jnp.int32)
    twos = (number_of - 1) // 2
    source_of, receiver = sizes[1:1 + 2 * twos:2], sizes[2:2 + 2 * twos:2]
    slack = jnp.minimum(source_of - 1, reach - receiver)
    moved = jax.random.randint(jax.random.fold_in(stream_key, 1), (twos,), 0, 1 << 20) % (slack + 1)
    sizes = sizes.at[1:1 + 2 * twos:2].set(source_of - moved).at[2:2 + 2 * twos:2].set(receiver + moved)
    return sizes[jax.random.permutation(jax.random.fold_in(stream_key, 2), number_of)]


def scatter_about(key, extent, scale, reach, cuts=(), dtype=jnp.bfloat16):
    gain = levels(key, extent, cuts, -0.22, 0.18) if cuts else 1.0
    values = jax.random.normal(key, extent, jnp.float32) * scale * gain
    return jnp.minimum(jnp.maximum(values, -reach), reach).astype(dtype)


def setup_inputs(seed: int = 0) -> dict:
    key_of = jax.random.split(jax.random.key(seed), 8)
    return {
        "controls": scatter_about(key_of[0], (MEMBERS, LEV, COLS), 1.0, 6.0, ((0, 8), (2, 64))),
        "perturbations": scatter_about(key_of[1], (MEMBERS, LEV, COLS), 1.0, 6.0, ((0, 8), (2, 64))),
        "vertical_filter": draw_vertical_filter(jax.random.fold_in(key_of[7], 71), 0),
        "scales": jnp.clip(jnp.exp(jax.random.uniform(key_of[3], (LEV,), jnp.float32, math.log(16.0), math.log(48.0))), 16.0, 48.0),
        "level_counts": uneven(key_of[4], TILES, LEV, SLOTS, 2).astype(jnp.int32),
        "weight_index": plant(jax.random.randint(key_of[5], (MEMBERS,), 0, NW), jax.random.fold_in(key_of[5], 1), 0, NW - 1).astype(jnp.int32),
        "member_weights": jnp.clip(jax.random.uniform(key_of[6], (NW,), jnp.float32, 0.1, 0.6), 0.1, 0.6),
    }


def tap_weights(scale):
    offsets = jnp.arange(-HALF, HALF + 1).astype(jnp.float32)
    width = scale[:, None]
    raw = jnp.exp(-(offsets * offsets) / (2.0 * width * width))
    normal = jnp.sqrt(lax.optimization_barrier(jnp.sum(jnp.exp(-(offsets * offsets) / (width * width)), axis=1, keepdims=True)))
    return raw / normal

def reference(controls, perturbations, vertical_filter, scales, level_counts, weight_index, member_weights):
    taps = tap_weights(scales).astype(jnp.bfloat16).astype(jnp.float32)
    betas = member_weights[weight_index]

    def one_member(total, inputs):
        control, perturb, weight = inputs
        lifted = jnp.dot(vertical_filter, control, preferred_element_type=jnp.float32).astype(jnp.bfloat16)
        lifted = lax.optimization_barrier(lifted).astype(jnp.float32).reshape(LEV, LAT, NLON)
        along = jnp.zeros((LEV, LAT, NLON), jnp.float32)
        for index in range(2 * HALF + 1):
            offset = index - HALF
            along = along + taps[:, index][:, None, None] * jnp.roll(lifted, offset, axis=2)
        along = lax.optimization_barrier(along.astype(jnp.bfloat16)).astype(jnp.float32)
        padded = jnp.pad(along, ((0, 0), (HALF, HALF), (0, 0)))
        smooth = jnp.zeros((LEV, LAT, NLON), jnp.float32)
        for index in range(2 * HALF + 1):
            offset = index - HALF
            smooth = smooth + taps[:, index][:, None, None] * padded[:, HALF - offset:HALF - offset + LAT, :]
        product = perturb.astype(jnp.float32).reshape(LEV, LAT, NLON) * smooth
        return (total + weight * product, None)
    total, _ = lax.scan(one_member, jnp.zeros((LEV, LAT, NLON), jnp.float32), (controls, perturbations, betas))
    increment = total.reshape(LEV, COLS)
    starts = (jnp.cumsum(level_counts) - level_counts).astype(jnp.int32)
    row_ids = jnp.arange(ROWS).astype(jnp.int32)
    owner = row_ids // SLOTS
    position = row_ids % SLOTS
    target = jnp.clip(starts[owner] + position, 0, LEV - 1).astype(jnp.int32)
    filled = position < level_counts[owner]
    slab = jnp.where(filled[:, None, None], total[target], jnp.float32(0.0))
    return (increment, slab)
```

```python
import jax
import jax.numpy as jnp
from jax import lax
from jax.experimental import pallas as pl
from jax.experimental.pallas import tpu as pltpu
from jax.sharding import PartitionSpec as P

LEV = 127
NLON = 1536
HALF = 24
MEM = 8
COL = 64
SIDE = 8
PARTS = 3
PAD = 32
MESH = pl.DeviceIdType.MESH
F32 = jnp.float32
BF16 = jnp.bfloat16


def taps_rows(width):
    rows = lax.broadcasted_iota(jnp.int32, (PAD, 128), 0).astype(F32)
    raw = jnp.exp(-(rows * rows) / (2.0 * width * width))
    squares = jnp.where(rows <= HALF, jnp.exp(-(rows * rows) / (width * width)), 0.0)
    normal = jnp.sqrt(2.0 * jnp.sum(squares, axis=0, keepdims=True) - 1.0)
    return (raw / normal).astype(BF16).astype(F32)


def placing_matrix(counts):
    row = lax.broadcasted_iota(jnp.int32, (COL * 8, 1), 0)
    tile, slot, half = row // 8, lax.rem(row, 4), lax.rem(row // 4, 2)
    lane = lax.broadcasted_iota(jnp.int32, (COL * 8, COL), 1)
    start = jnp.sum(jnp.where(lane < tile, counts, 0.0), axis=1, keepdims=True)
    count = jnp.sum(jnp.where(lane == tile, counts, 0.0), axis=1, keepdims=True)
    slot_f = slot.astype(F32)
    target = jnp.where(slot_f < count, start + slot_f + 128.0 * half.astype(F32), -1.0)
    wide = lax.broadcasted_iota(jnp.int32, (COL * 8, 256), 1).astype(F32)
    return jnp.where(wide == target, 1.0, 0.0).astype(BF16)


def exchange_kernel(
    controls, perturb, vertical, scales, counts, index, weights,
    gathered_out, slab_out,
    lifted, width_row, taps, along, arrived, padded, smooth, back, scaled,
    terms, sums, total, gathered, pair, placing, slab_send, slab_recv,
    send_sems, recv_sems,
):
    m = lax.axis_index("mem")
    c = lax.axis_index("col")
    z, y = c // SIDE, lax.rem(c, SIDE)

    barrier = pltpu.get_barrier_semaphore()

    def greet(k, carry):
        pl.semaphore_signal(
            barrier, inc=1, device_id=(m, lax.rem(c + k, COL)), device_id_type=MESH
        )
        return carry

    lax.fori_loop(1, COL, greet, 0)
    for k in range(1, MEM):
        pl.semaphore_signal(barrier, inc=1, device_id=(lax.rem(m + k, MEM), c), device_id_type=MESH)

    width_row[...] = jnp.full((1, 128), 16.0, F32)
    width_row[:, :LEV] = scales[...]
    taps[...] = taps_rows(width_row[...])

    def lift(matrix, source, t):
        block = jnp.dot(
            matrix, source[0, :, pl.ds(pl.multiple_of(t * 128, 128), 128)],
            preferred_element_type=F32,
        )
        return block

    filter_rows = vertical[...]

    def lift_block(t, carry):
        block = lift(filter_rows, controls, t).astype(BF16).astype(F32)
        lifted[pl.ds(pl.multiple_of(PAD + t * 128, 32), 128), :] = block.T
        return carry

    lax.fori_loop(0, NLON // 128, lift_block, 0)
    lifted[pl.ds(0, PAD), :] = lifted[pl.ds(NLON, PAD), :]
    lifted[pl.ds(PAD + NLON, PAD), :] = lifted[pl.ds(PAD, PAD), :]
    padded[pl.ds(0, HALF)] = jnp.zeros((HALF, 8, 128), F32)
    padded[pl.ds(HALF + COL, HALF)] = jnp.zeros((HALF, 8, 128), F32)

    pl.semaphore_wait(barrier, COL - 1 + MEM - 1)

    def weight_rows():
        return [jnp.broadcast_to(taps[k : k + 1, :], (8, 128)) for k in range(HALF + 1)]

    def send_col(kind, s, src, dst, row):
        pltpu.make_async_remote_copy(
            src_ref=src, dst_ref=dst,
            send_sem=send_sems.at[kind, s], recv_sem=recv_sems.at[kind, s],
            device_id=(m, row), device_id_type=MESH,
        ).start()

    def send_group(kind, s, source, dest, group, other):
        for r in range(SIDE):
            row = group * SIDE + lax.rem(y + r, SIDE)
            if r == 0:
                @pl.when(other)
                def _():
                    send_col(kind, s, source.at[s, row], dest.at[s, c], row)
            else:
                send_col(kind, s, source.at[s, row], dest.at[s, c], row)

    def lon_step(it, carry):
        w = weight_rows()
        s, k = it // SIDE, lax.rem(it, SIDE)
        group = lax.rem(z + 4 + k, SIDE)
        base = PAD + group * 192 + s * 64
        for b in range(SIDE):
            at = pl.multiple_of(base + 8 * b, 8)
            acc = w[0] * lifted[pl.ds(at, 8), :]
            for tap in range(1, HALF + 1):
                acc = acc + w[tap] * (lifted[pl.ds(at - tap, 8), :] + lifted[pl.ds(at + tap, 8), :])
            along[s, group * SIDE + b] = acc.astype(BF16)
        send_group(0, s, along, arrived, group, k != 4)
        return carry

    lax.fori_loop(0, PARTS * SIDE, lon_step, 0)

    beta = weights[index[0]]
    identity = jnp.where(
        lax.broadcasted_iota(jnp.int32, (128, LEV), 0)
        == lax.broadcasted_iota(jnp.int32, (128, LEV), 1),
        1.0, 0.0,
    ).astype(BF16)

    def perturb_block(t, carry):
        block = lift(identity, perturb, t) * beta
        scaled[pl.ds(pl.multiple_of(t * 128, 128), 128), :] = block.T
        return carry

    lax.fori_loop(0, NLON // 128, perturb_block, 0)
    placing[...] = placing_matrix(counts[...])
    pair[pl.ds(64, 64), pl.ds(128, 128)] = jnp.zeros((64, 128), BF16)

    def wait_recv(kind, s, dest, count):
        ref = dest.at[s, pl.ds(0, count)]
        pltpu.make_async_remote_copy(
            src_ref=ref, dst_ref=ref,
            send_sem=send_sems.at[kind, s], recv_sem=recv_sems.at[kind, s],
            device_id=(m, c), device_id_type=MESH,
        ).wait_recv()

    def wait_send(kind, s, source, count):
        ref = source.at[s, pl.ds(0, count)]
        pltpu.make_async_remote_copy(
            src_ref=ref, dst_ref=ref,
            send_sem=send_sems.at[kind, s], recv_sem=recv_sems.at[kind, s],
            device_id=(m, c), device_id_type=MESH,
        ).wait_send()

    def lat_part(s, carry):
        wait_recv(0, s, arrived, COL - 1)
        arrived[s, c] = along[s, c]
        padded[pl.ds(HALF, COL)] = arrived[s].astype(F32)

        def lat_step(k, inner):
            w = weight_rows()
            group = lax.rem(z + 4 + k, SIDE)
            for r in range(SIDE):
                at = HALF + group * SIDE + r
                acc = w[0] * padded[at]
                for tap in range(1, HALF + 1):
                    acc = acc + w[tap] * (padded[at - tap] + padded[at + tap])
                smooth[s, group * SIDE + r] = acc.astype(BF16)
            send_group(1, s, smooth, back, group, k != 4)
            return inner

        lax.fori_loop(0, SIDE, lat_step, 0)
        return carry

    lax.fori_loop(0, PARTS, lat_part, 0)

    def product_part(s, carry):
        wait_recv(1, s, back, COL - 1)
        back[s, c] = smooth[s, c]

        def product_step(k, inner):
            j = lax.rem(m + 1 + k, MEM)
            field = back[s, pl.ds(j * SIDE, SIDE)].astype(F32).reshape(64, 128)
            rows = scaled[pl.ds(pl.multiple_of(j * 192 + s * 64, 64), 64), :]
            terms[s, j] = (field * rows).astype(BF16).reshape(8, 8, 128)

            @pl.when(k < MEM - 1)
            def _():
                pltpu.make_async_remote_copy(
                    src_ref=terms.at[s, j], dst_ref=sums.at[s, m],
                    send_sem=send_sems.at[2, s], recv_sem=recv_sems.at[2, s],
                    device_id=(j, c), device_id_type=MESH,
                ).start()

            return inner

        lax.fori_loop(0, MEM, product_step, 0)
        return carry

    def sum_part(s, carry):
        wait_recv(2, s, sums, MEM - 1)
        sums[s, m] = terms[s, m]
        acc = sums[s, 0].astype(F32)
        for k in range(1, MEM):
            acc = acc + sums[s, k].astype(F32)
        part = acc.astype(BF16)
        total[s] = part
        gathered[s, m] = part

        def spread(k, inner):
            pltpu.make_async_remote_copy(
                src_ref=total.at[s], dst_ref=gathered.at[s, m],
                send_sem=send_sems.at[3, s], recv_sem=recv_sems.at[3, s],
                device_id=(lax.rem(m + k, MEM), c), device_id_type=MESH,
            ).start()
            return inner

        lax.fori_loop(1, MEM, spread, 0)
        return carry

    def product_sum(s, carry):
        product_part(s, 0)

        @pl.when(s > 0)
        def _():
            sum_part(s - 1, 0)

        return carry

    lax.fori_loop(0, PARTS, product_sum, 0)
    sum_part(PARTS - 1, 0)

    pair[pl.ds(0, 64), pl.ds(0, 128)] = total[0].reshape(64, 128)
    pair[pl.ds(64, 64), pl.ds(0, 128)] = total[1].reshape(64, 128)
    pair[pl.ds(0, 64), pl.ds(128, 128)] = total[2].reshape(64, 128)
    slab_send[0] = (
        lax.dot_general(
            placing[...], pair[...], (((1,), (1,)), ((), ())), preferred_element_type=F32
        )
        .astype(BF16)
        .reshape(COL, 8, 128)
    )

    def slab_step(k, carry):
        group = lax.rem(z + 4 + k, SIDE)
        for r in range(SIDE):
            row = group * SIDE + lax.rem(y + r, SIDE)
            if r == 0:
                @pl.when(k != 4)
                def _():
                    send_col(4, 0, slab_send.at[0, row], slab_recv.at[0, c], row)
            else:
                send_col(4, 0, slab_send.at[0, row], slab_recv.at[0, c], row)
        return carry

    lax.fori_loop(0, SIDE, slab_step, 0)

    def finish(s, carry):
        wait_recv(3, s, gathered, MEM - 1)
        gathered_out[s] = gathered[s]
        wait_send(0, s, along, COL - 1)
        wait_send(1, s, smooth, COL - 1)
        wait_send(2, s, terms, MEM - 1)
        wait_send(3, s, terms, MEM - 1)
        return carry

    lax.fori_loop(0, PARTS, finish, 0)
    wait_recv(4, 0, slab_recv, COL - 1)
    slab_recv[0, c] = slab_send[0, c]
    slab_out[...] = slab_recv[0]
    wait_send(4, 0, slab_send, COL - 1)


def exchange(controls, perturb, vertical, scales, counts, index, weights):
    block = (8, 128)
    vmem = pl.BlockSpec(memory_space=pltpu.VMEM)
    smem = pl.BlockSpec(memory_space=pltpu.SMEM)
    return pl.pallas_call(
        exchange_kernel,
        out_shape=(
            jax.ShapeDtypeStruct((PARTS, MEM, 8) + block, BF16),
            jax.ShapeDtypeStruct((COL,) + block, BF16),
        ),
        in_specs=[vmem, vmem, vmem, vmem, vmem, smem, smem],
        out_specs=(vmem, vmem),
        scratch_shapes=[
            pltpu.VMEM((PAD + NLON + PAD, 128), F32),
            pltpu.VMEM((1, 128), F32),
            pltpu.VMEM((PAD, 128), F32),
            pltpu.VMEM((PARTS, COL) + block, BF16),
            pltpu.VMEM((PARTS, COL) + block, BF16),
            pltpu.VMEM((HALF + COL + HALF,) + block, F32),
            pltpu.VMEM((PARTS, COL) + block, BF16),
            pltpu.VMEM((PARTS, COL) + block, BF16),
            pltpu.VMEM((NLON, 128), F32),
            pltpu.VMEM((PARTS, MEM, 8) + block, BF16),
            pltpu.VMEM((PARTS, MEM, 8) + block, BF16),
            pltpu.VMEM((PARTS, 8) + block, BF16),
            pltpu.VMEM((PARTS, MEM, 8) + block, BF16),
            pltpu.VMEM((128, 256), BF16),
            pltpu.VMEM((COL * 8, 256), BF16),
            pltpu.VMEM((1, COL) + block, BF16),
            pltpu.VMEM((1, COL) + block, BF16),
            pltpu.SemaphoreType.DMA((5, PARTS)),
            pltpu.SemaphoreType.DMA((5, PARTS)),
        ],
        compiler_params=pltpu.CompilerParams(
            collective_id=0, has_side_effects=True, vmem_limit_bytes=40 * 1024 * 1024
        ),
        name="exchange",
    )(controls, perturb, vertical, scales, counts, index, weights)


def arrange_kernel(gathered, slab, increment, slab_increment, rows):
    for t in range(NLON // 128):
        halves = [gathered[u % 3, u // 3].astype(F32).reshape(64, 128) for u in (2 * t, 2 * t + 1)]
        block = jnp.concatenate(halves, axis=0).T
        increment[:, pl.ds(t * 128, 128)] = block[:LEV]
    rows[...] = slab[...].astype(F32).reshape(COL * 8, 128)
    for q in range(4):
        slab_increment[q, :, pl.ds(0, 128)] = rows[pl.ds(q, COL, stride=8), :]
        slab_increment[q, :, pl.ds(128, 64)] = rows[pl.ds(4 + q, COL, stride=8), :][:, :64]


def arrange(gathered, slab):
    vmem = pl.BlockSpec(memory_space=pltpu.VMEM)
    return pl.pallas_call(
        arrange_kernel,
        out_shape=(
            jax.ShapeDtypeStruct((LEV, NLON), F32),
            jax.ShapeDtypeStruct((4, COL, 192), F32),
        ),
        in_specs=[vmem, vmem],
        out_specs=(vmem, vmem),
        scratch_shapes=[pltpu.VMEM((COL * 8, 128), F32)],
        compiler_params=pltpu.CompilerParams(vmem_limit_bytes=16 * 1024 * 1024),
        name="arrange",
    )(gathered, slab)


def on_device(
    controls, perturbations, vertical_filter, scales, level_counts, weight_index, member_weights
):
    vertical = jnp.pad(vertical_filter, ((0, 1), (0, 0)))
    gathered, slab = exchange(
        controls, perturbations, vertical, scales[None, :],
        level_counts.astype(F32)[None, :], weight_index, member_weights,
    )
    return arrange(gathered, slab)


def solution(mesh):
    return jax.shard_map(
        on_device,
        mesh=mesh,
        in_specs=(P("mem", None, "col"), P("mem", None, "col"), P(), P(), P(), P("mem"), P()),
        out_specs=(P(None, "col"), P("col", None, "mem")),
        check_vma=False,
    )
```

```python
import jax
import jax.numpy as jnp
from jax import lax
from jax.experimental import pallas as pl
from jax.experimental.pallas import tpu as pltpu
from jax.sharding import PartitionSpec as P

LEV = 127
NLON = 1536
HALF = 24
MEM = 8
COL = 64
SIDE = 8
PARTS = 3
PAD = 32
MESH = pl.DeviceIdType.MESH
F32 = jnp.float32
BF16 = jnp.bfloat16


def taps_rows(width):
    rows = lax.broadcasted_iota(jnp.int32, (PAD, 128), 0).astype(F32)
    raw = jnp.exp(-(rows * rows) / (2.0 * width * width))
    squares = jnp.where(rows <= HALF, jnp.exp(-(rows * rows) / (width * width)), 0.0)
    normal = jnp.sqrt(2.0 * jnp.sum(squares, axis=0, keepdims=True) - 1.0)
    return (raw / normal).astype(BF16).astype(F32)


def placing_matrices(counts):
    def starts_counts(tile, rows):
        lane = lax.broadcasted_iota(jnp.int32, (rows, COL), 1)
        start = jnp.sum(jnp.where(lane < tile, counts, 0.0), axis=1, keepdims=True)
        count = jnp.sum(jnp.where(lane == tile, counts, 0.0), axis=1, keepdims=True)
        return start, count

    row = lax.broadcasted_iota(jnp.int32, (COL * 4, 1), 0)
    start, count = starts_counts(row // 4, COL * 4)
    slot = lax.rem(row, 4).astype(F32)
    target = jnp.where(slot < count, start + slot, -1.0)
    lane = lax.broadcasted_iota(jnp.int32, (COL * 4, 128), 1).astype(F32)
    first = jnp.where(lane == target, 1.0, 0.0).astype(BF16)
    row = lax.broadcasted_iota(jnp.int32, (COL * 2, 1), 0)
    start, count = starts_counts(row // 2, COL * 2)
    lane = lax.broadcasted_iota(jnp.int32, (COL * 2, 128), 1).astype(F32)
    both = []
    for odd in range(2):
        slot = (2 * lax.rem(row, 2) + odd).astype(F32)
        target = jnp.where(slot < count, start + slot, -1.0)
        both.append(jnp.where(lane == target, 1.0, 0.0).astype(BF16))
    return first, both[0], both[1]


def exchange_kernel(
    controls_hbm, perturb_hbm, vertical_hbm, scales_hbm, counts_hbm, index_hbm, weights_hbm,
    gathered_out, slab_a_out, slab_b_out,
    controls, perturb, vertical, scales, counts, index, weights,
    matrix_rows, lifted, width_row, taps, along, arrived, padded, smooth, back, columns, members,
    total, gathered, pair_a, pair_b, place_a, place_b,
    send_a, recv_a, send_b, recv_b,
    send_sems, recv_sems, load_sems,
):
    m = lax.axis_index("mem")
    c = lax.axis_index("col")
    z, y = c // SIDE, lax.rem(c, SIDE)

    loads = [
        pltpu.make_async_copy(src, dst, load_sems.at[k])
        for k, (src, dst) in enumerate(
            (
                (vertical_hbm, vertical), (controls_hbm, controls), (scales_hbm, scales),
                (counts_hbm, counts), (index_hbm, index), (weights_hbm, weights),
                (perturb_hbm, perturb),
            )
        )
    ]
    for load in loads:
        load.start()

    barrier = pltpu.get_barrier_semaphore()
    for a in (4, 3, 5, 2, 6, 1, 7, 0):
        zz = lax.rem(z + a, SIDE) * SIDE
        for b in (4, 3, 5, 2, 6, 1, 7, 0):
            if a or b:
                pl.semaphore_signal(
                    barrier, inc=1, device_id=(m, zz + lax.rem(y + b, SIDE)), device_id_type=MESH
                )
    for k in range(1, MEM):
        pl.semaphore_signal(barrier, inc=1, device_id=(lax.rem(m + k, MEM), c), device_id_type=MESH)

    matrix_rows[pl.ds(LEV, 1), :] = jnp.zeros((1, LEV), F32)
    loads[0].wait()
    matrix_rows[pl.ds(0, LEV), :] = vertical[...].astype(F32)
    filter_rows = matrix_rows[...].astype(BF16)
    loads[1].wait()
    for t in range(NLON // 128):
        block = jnp.dot(
            filter_rows, controls[0, :, pl.ds(t * 128, 128)], preferred_element_type=F32
        )
        lifted[pl.ds(PAD + t * 128, 128), :] = block.astype(BF16).astype(F32).T
    lifted[pl.ds(0, PAD), :] = lifted[pl.ds(NLON, PAD), :]
    lifted[pl.ds(PAD + NLON, PAD), :] = lifted[pl.ds(PAD, PAD), :]

    width_row[...] = jnp.full((1, 128), 16.0, F32)
    loads[2].wait()
    width_row[:, :LEV] = scales[...]
    taps[...] = taps_rows(width_row[...])
    padded[pl.ds(0, HALF)] = jnp.zeros((HALF, 8, 128), F32)
    padded[pl.ds(HALF + COL, HALF)] = jnp.zeros((HALF, 8, 128), F32)

    def weight_rows():
        return [jnp.broadcast_to(taps[k : k + 1, :], (8, 128)) for k in range(HALF + 1)]

    def send(kind, s, src, dst, device):
        pltpu.make_async_remote_copy(
            src_ref=src, dst_ref=dst,
            send_sem=send_sems.at[kind, s], recv_sem=recv_sems.at[kind, s],
            device_id=device, device_id_type=MESH,
        ).start()

    def whole(kind, s, ref, count):
        part = ref.at[s, pl.ds(0, count)]
        return pltpu.make_async_remote_copy(
            src_ref=part, dst_ref=part,
            send_sem=send_sems.at[kind, s], recv_sem=recv_sems.at[kind, s],
            device_id=(m, c), device_id_type=MESH,
        )

    def send_group(kind, s, source, dest, slot, member, group, away):
        for r in range(SIDE):
            row = group * SIDE + lax.rem(y + r, SIDE)
            if away is True:
                send(kind, s, source.at[s, row], dest.at[s, slot], (member, row))
            elif away is False:
                if r:
                    send(kind, s, source.at[s, row], dest.at[s, slot], (member, row))
            elif r == 0:
                @pl.when(away)
                def _():
                    send(kind, s, source.at[s, row], dest.at[s, slot], (member, row))
            else:
                send(kind, s, source.at[s, row], dest.at[s, slot], (member, row))

    def lon_filter(s, group):
        w = weight_rows()
        base = PAD + group * 192 + s * 64
        for b in range(SIDE):
            at = pl.multiple_of(base + 8 * b, 8)
            acc = w[0] * lifted[pl.ds(at, 8), :]
            for tap in range(1, HALF + 1):
                acc = acc + w[tap] * (lifted[pl.ds(at - tap, 8), :] + lifted[pl.ds(at + tap, 8), :])
            along[s, group * SIDE + b] = acc.astype(BF16)

    def lon_first(k, carry):
        lon_filter(0, lax.rem(z + 4 + k, SIDE))
        return carry

    lax.fori_loop(0, SIDE, lon_first, 0)
    pl.semaphore_wait(barrier, COL - 1 + MEM - 1)

    for k in range(SIDE):
        send_group(0, 0, along, arrived, c, m, lax.rem(z + 4 + k, SIDE), k != 4)

    def lon_step(it, carry):
        s, k = it // SIDE, lax.rem(it, SIDE)
        group = lax.rem(z + 4 + k, SIDE)
        lon_filter(s, group)
        send_group(0, s, along, arrived, c, m, group, k != 4)
        return carry

    lax.fori_loop(SIDE, PARTS * SIDE, lon_step, 0)

    identity = jnp.where(
        lax.broadcasted_iota(jnp.int32, (128, LEV), 0)
        == lax.broadcasted_iota(jnp.int32, (128, LEV), 1),
        1.0, 0.0,
    ).astype(BF16)
    for k in range(3, 7):
        loads[k].wait()
    beta = weights[index[0]]
    for t in range(NLON // 128):
        block = jnp.dot(identity, perturb[0, :, pl.ds(t * 128, 128)], preferred_element_type=F32)
        block = block.T.astype(BF16).reshape(2, 8, 8, 128)
        for half in range(2):
            u = 2 * t + half
            columns[0, u // 3, u % 3] = block[half]
    for k in (4, 3, 5, 2, 6, 1, 7):
        j = lax.rem(m + k, MEM)
        send(2, 0, columns.at[0, j], members.at[0, m], (j, c))
    members[0, m] = columns[0, m]
    first, even, odd = placing_matrices(counts[...].astype(F32))
    place_a[...] = first
    place_b[:, pl.ds(0, 128)] = even
    place_b[:, pl.ds(128, 128)] = odd
    pair_b[pl.ds(0, 64), pl.ds(128, 128)] = jnp.zeros((64, 128), BF16)
    pair_b[pl.ds(64, 64), pl.ds(0, 128)] = jnp.zeros((64, 128), BF16)

    here = z == m
    back_slot = m * SIDE + y
    taps[...] = taps[...] * beta

    def lat_part(s, carry):
        whole(0, s, arrived, COL - 1).wait_recv()
        arrived[s, c] = along[s, c]
        padded[pl.ds(HALF, COL)] = arrived[s].astype(F32)

        def lat_step(k, inner):
            w = weight_rows()
            group = lax.rem(z + 4 + k, SIDE)
            for r in range(SIDE):
                at = HALF + group * SIDE + r
                acc = w[0] * padded[at]
                for tap in range(1, HALF + 1):
                    acc = acc + w[tap] * (padded[at - tap] + padded[at + tap])
                smooth[s, group * SIDE + r] = acc.astype(BF16)
            send_group(
                1, s, smooth, back, back_slot, z, group,
                jnp.logical_or(k != 4, jnp.logical_not(here)),
            )
            return inner

        lax.fori_loop(0, SIDE, lat_step, 0)
        return carry

    lax.fori_loop(0, PARTS, lat_part, 0)
    whole(2, 0, members, MEM - 1).wait_recv()

    def sum_part(s):
        @pl.when(here)
        def _():
            whole(1, s, back, COL - 1).wait_recv()
            back[s, back_slot] = smooth[s, c]

        @pl.when(jnp.logical_not(here))
        def _():
            whole(1, s, back, COL).wait_recv()

        acc = jnp.zeros((8, 8, 128), F32)
        for k in range(MEM):
            acc = acc + back[s, pl.ds(k * SIDE, SIDE)].astype(F32) * members[0, k, s].astype(F32)
        total[s] = acc.astype(BF16)
        gathered[s, m] = total[s]

    def spread_part(s):
        for k in (4, 3, 5, 2, 6, 1, 7):
            send(3, s, total.at[s], gathered.at[s, m], (lax.rem(m + k, MEM), c))

    def slab_part(kind, place, pair, source, dest, rows):
        source[0] = (
            lax.dot_general(
                place[...], pair[...], (((1,), (1,)), ((), ())), preferred_element_type=F32
            )
            .astype(BF16)
            .reshape(COL, rows, 128)
        )

        for k in range(SIDE):
            group = lax.rem(z + 4 + k, SIDE)
            send_group(kind, 0, source, dest, c, m, group, k != 4)

    sum_part(0)
    spread_part(0)
    sum_part(1)
    spread_part(1)
    pair_a[pl.ds(0, 64), :] = total[0].reshape(64, 128)
    pair_a[pl.ds(64, 64), :] = total[1].reshape(64, 128)
    slab_part(4, place_a, pair_a, send_a, recv_a, 4)
    sum_part(2)
    last = total[2].reshape(64, 128)
    pair_b[pl.ds(0, 64), pl.ds(0, 128)] = last
    pair_b[pl.ds(64, 64), pl.ds(128, 128)] = last
    slab_part(5, place_b, pair_b, send_b, recv_b, 2)
    spread_part(2)

    def finish(s, carry):
        whole(3, s, gathered, MEM - 1).wait_recv()
        gathered_out[s] = gathered[s]
        whole(0, s, along, COL - 1).wait_send()

        @pl.when(here)
        def _():
            whole(1, s, smooth, COL - 1).wait_send()

        @pl.when(jnp.logical_not(here))
        def _():
            whole(1, s, smooth, COL).wait_send()

        whole(3, s, gathered, MEM - 1).wait_send()
        return carry

    lax.fori_loop(0, PARTS, finish, 0)
    whole(2, 0, columns, MEM - 1).wait_send()
    whole(4, 0, recv_a, COL - 1).wait_recv()
    recv_a[0, c] = send_a[0, c]
    slab_a_out[...] = recv_a[0]
    whole(5, 0, recv_b, COL - 1).wait_recv()
    recv_b[0, c] = send_b[0, c]
    slab_b_out[...] = recv_b[0]
    whole(4, 0, send_a, COL - 1).wait_send()
    whole(5, 0, send_b, COL - 1).wait_send()


def exchange(controls, perturb, vertical, scales, counts, index, weights):
    block = (8, 128)
    vmem = pl.BlockSpec(memory_space=pltpu.VMEM)
    hbm = pl.BlockSpec(memory_space=pl.ANY)
    return pl.pallas_call(
        exchange_kernel,
        out_shape=(
            jax.ShapeDtypeStruct((PARTS, MEM, 8) + block, BF16),
            jax.ShapeDtypeStruct((COL, 4, 128), BF16),
            jax.ShapeDtypeStruct((COL, 2, 128), BF16),
        ),
        in_specs=[hbm] * 7,
        out_specs=(vmem, vmem, vmem),
        scratch_shapes=[
            pltpu.VMEM((1, LEV, NLON), BF16),
            pltpu.VMEM((1, LEV, NLON), BF16),
            pltpu.VMEM((LEV, LEV), BF16),
            pltpu.VMEM((1, LEV), F32),
            pltpu.VMEM((1, COL), jnp.int32),
            pltpu.SMEM((1,), jnp.int32),
            pltpu.SMEM((10,), F32),
            pltpu.VMEM((128, LEV), F32),
            pltpu.VMEM((PAD + NLON + PAD, 128), F32),
            pltpu.VMEM((1, 128), F32),
            pltpu.VMEM((PAD, 128), F32),
            pltpu.VMEM((PARTS, COL) + block, BF16),
            pltpu.VMEM((PARTS, COL) + block, BF16),
            pltpu.VMEM((HALF + COL + HALF,) + block, F32),
            pltpu.VMEM((PARTS, COL) + block, BF16),
            pltpu.VMEM((PARTS, COL) + block, BF16),
            pltpu.VMEM((1, MEM, PARTS, 8) + block, BF16),
            pltpu.VMEM((1, MEM, PARTS, 8) + block, BF16),
            pltpu.VMEM((PARTS, 8) + block, BF16),
            pltpu.VMEM((PARTS, MEM, 8) + block, BF16),
            pltpu.VMEM((128, 128), BF16),
            pltpu.VMEM((128, 256), BF16),
            pltpu.VMEM((COL * 4, 128), BF16),
            pltpu.VMEM((COL * 2, 256), BF16),
            pltpu.VMEM((1, COL, 4, 128), BF16),
            pltpu.VMEM((1, COL, 4, 128), BF16),
            pltpu.VMEM((1, COL, 2, 128), BF16),
            pltpu.VMEM((1, COL, 2, 128), BF16),
            pltpu.SemaphoreType.DMA((6, PARTS)),
            pltpu.SemaphoreType.DMA((6, PARTS)),
            pltpu.SemaphoreType.DMA((7,)),
        ],
        compiler_params=pltpu.CompilerParams(
            collective_id=0, has_side_effects=True, vmem_limit_bytes=32 * 1024 * 1024
        ),
        name="exchange",
    )(
        *(
            pltpu.with_memory_space_constraint(x, pltpu.HBM)
            for x in (controls, perturb, vertical, scales, counts)
        ),
        index, pltpu.with_memory_space_constraint(weights, pltpu.HBM),
    )


def arrange_kernel(gathered, slab_a, slab_b, increment, slab_increment, rows_a, rows_b):
    for t in range(NLON // 128):
        halves = [gathered[u % 3, u // 3].astype(F32).reshape(64, 128) for u in (2 * t, 2 * t + 1)]
        block = jnp.concatenate(halves, axis=0).T
        increment[:, pl.ds(t * 128, 128)] = block[:LEV]
    rows_a[...] = slab_a[...].astype(F32).reshape(COL * 4, 128)
    rows_b[...] = slab_b[...].astype(F32).reshape(COL * 2, 128)
    for q in range(4):
        slab_increment[q, :, pl.ds(0, 128)] = rows_a[pl.ds(q, COL, stride=4), :]
    for r in range(2):
        both = rows_b[pl.ds(r, COL, stride=2), :]
        slab_increment[2 * r, :, pl.ds(128, 64)] = both[:, :64]
        slab_increment[2 * r + 1, :, pl.ds(128, 64)] = both[:, 64:]


def arrange(gathered, slab_a, slab_b):
    vmem = pl.BlockSpec(memory_space=pltpu.VMEM)
    return pl.pallas_call(
        arrange_kernel,
        out_shape=(
            jax.ShapeDtypeStruct((LEV, NLON), F32),
            jax.ShapeDtypeStruct((4, COL, 192), F32),
        ),
        in_specs=[vmem, vmem, vmem],
        out_specs=(vmem, vmem),
        scratch_shapes=[pltpu.VMEM((COL * 4, 128), F32), pltpu.VMEM((COL * 2, 128), F32)],
        compiler_params=pltpu.CompilerParams(vmem_limit_bytes=16 * 1024 * 1024),
        name="arrange",
    )(gathered, slab_a, slab_b)


def on_device(
    controls, perturbations, vertical_filter, scales, level_counts, weight_index, member_weights
):
    outs = exchange(
        controls, perturbations, vertical_filter, scales[None, :],
        level_counts[None, :], weight_index, member_weights,
    )
    return arrange(*outs)


def solution(mesh):
    return jax.shard_map(
        on_device,
        mesh=mesh,
        in_specs=(P("mem", None, "col"), P("mem", None, "col"), P(), P(), P(), P("mem"), P()),
        out_specs=(P(None, "col"), P("col", None, "mem")),
        check_vma=False,
    )
```

```python
import jax
import jax.numpy as jnp
from jax import lax
from jax.experimental import pallas as pl
from jax.experimental.pallas import tpu as pltpu
from jax.sharding import PartitionSpec as P

LEV = 127
NLON = 1536
HALF = 24
MEM = 8
COL = 64
SIDE = 8
PARTS = 3
PAD = 32
MESH = pl.DeviceIdType.MESH
FAR_FIRST = (4, 3, 5, 2, 6, 1, 7, 0)
F32 = jnp.float32
BF16 = jnp.bfloat16


def taps_rows(width):
    rows = lax.broadcasted_iota(jnp.int32, (PAD, 128), 0).astype(F32)
    raw = jnp.exp(-(rows * rows) / (2.0 * width * width))
    squares = jnp.where(rows <= HALF, jnp.exp(-(rows * rows) / (width * width)), 0.0)
    normal = jnp.sqrt(2.0 * jnp.sum(squares, axis=0, keepdims=True) - 1.0)
    return (raw / normal).astype(BF16).astype(F32)


def placing_matrices(counts):
    def starts_counts(tile, rows):
        lane = lax.broadcasted_iota(jnp.int32, (rows, COL), 1)
        start = jnp.sum(jnp.where(lane < tile, counts, 0.0), axis=1, keepdims=True)
        count = jnp.sum(jnp.where(lane == tile, counts, 0.0), axis=1, keepdims=True)
        return start, count

    row = lax.broadcasted_iota(jnp.int32, (COL * 4, 1), 0)
    start, count = starts_counts(row // 4, COL * 4)
    slot = lax.rem(row, 4).astype(F32)
    target = jnp.where(slot < count, start + slot, -1.0)
    lane = lax.broadcasted_iota(jnp.int32, (COL * 4, 128), 1).astype(F32)
    first = jnp.where(lane == target, 1.0, 0.0).astype(BF16)
    row = lax.broadcasted_iota(jnp.int32, (COL * 2, 1), 0)
    start, count = starts_counts(row // 2, COL * 2)
    lane = lax.broadcasted_iota(jnp.int32, (COL * 2, 128), 1).astype(F32)
    both = []
    for odd in range(2):
        slot = (2 * lax.rem(row, 2) + odd).astype(F32)
        target = jnp.where(slot < count, start + slot, -1.0)
        both.append(jnp.where(lane == target, 1.0, 0.0).astype(BF16))
    return first, both[0], both[1]


def exchange_kernel(
    controls_hbm, perturb_hbm, vertical_hbm, scales_hbm, counts_hbm, index_hbm, weights_hbm,
    increment_out, slab_a_out, slab_b_out,
    controls, perturb, vertical, scales, counts, index, weights,
    matrix_rows, lifted, width_row, taps, along, arrived, padded, smooth, back, columns, members,
    total, gathered, pair_a, pair_b, place_a, place_b,
    send_a, recv_a, send_b, recv_b,
    send_sems, recv_sems, load_sems,
):
    m = lax.axis_index("mem")
    c = lax.axis_index("col")
    z, y = c // SIDE, lax.rem(c, SIDE)

    loads = [
        pltpu.make_async_copy(src, dst, load_sems.at[k])
        for k, (src, dst) in enumerate(
            (
                (vertical_hbm, vertical), (controls_hbm, controls), (scales_hbm, scales),
                (counts_hbm, counts), (index_hbm, index), (weights_hbm, weights),
                (perturb_hbm, perturb),
            )
        )
    ]
    for load in loads:
        load.start()

    barrier = pltpu.get_barrier_semaphore()
    for a in FAR_FIRST:
        zz = lax.rem(z + a, SIDE) * SIDE
        for b in FAR_FIRST:
            if a or b:
                pl.semaphore_signal(
                    barrier, inc=1, device_id=(m, zz + lax.rem(y + b, SIDE)), device_id_type=MESH
                )
    for k in range(1, MEM):
        pl.semaphore_signal(barrier, inc=1, device_id=(lax.rem(m + k, MEM), c), device_id_type=MESH)

    matrix_rows[pl.ds(LEV, 1), :] = jnp.zeros((1, LEV), F32)
    loads[0].wait()
    matrix_rows[pl.ds(0, LEV), :] = vertical[...].astype(F32)
    filter_rows = matrix_rows[...].astype(BF16)
    loads[1].wait()
    for t in range(NLON // 128):
        block = jnp.dot(
            filter_rows, controls[0, :, pl.ds(t * 128, 128)], preferred_element_type=F32
        )
        lifted[pl.ds(PAD + t * 128, 128), :] = block.astype(BF16).astype(F32).T
    lifted[pl.ds(0, PAD), :] = lifted[pl.ds(NLON, PAD), :]
    lifted[pl.ds(PAD + NLON, PAD), :] = lifted[pl.ds(PAD, PAD), :]

    width_row[...] = jnp.full((1, 128), 16.0, F32)
    loads[2].wait()
    width_row[:, :LEV] = scales[...]
    taps[...] = taps_rows(width_row[...])
    padded[pl.ds(0, HALF)] = jnp.zeros((HALF, 8, 128), F32)
    padded[pl.ds(HALF + COL, HALF)] = jnp.zeros((HALF, 8, 128), F32)

    def weight_rows():
        return [jnp.broadcast_to(taps[k : k + 1, :], (8, 128)) for k in range(HALF + 1)]

    def send(kind, s, src, dst, device):
        pltpu.make_async_remote_copy(
            src_ref=src, dst_ref=dst,
            send_sem=send_sems.at[kind, s], recv_sem=recv_sems.at[kind, s],
            device_id=device, device_id_type=MESH,
        ).start()

    def whole(kind, s, ref, count):
        part = ref.at[s, pl.ds(0, count)]
        return pltpu.make_async_remote_copy(
            src_ref=part, dst_ref=part,
            send_sem=send_sems.at[kind, s], recv_sem=recv_sems.at[kind, s],
            device_id=(m, c), device_id_type=MESH,
        )

    def send_group(kind, s, source, dest, slot, member, group, away):
        for b in FAR_FIRST:
            row = group * SIDE + lax.rem(y + b, SIDE)
            if b or away is True:
                send(kind, s, source.at[s, row], dest.at[s, slot], (member, row))
            elif away is not False:
                @pl.when(away)
                def _():
                    send(kind, s, source.at[s, row], dest.at[s, slot], (member, row))

    def group_at(k):
        return lax.rem(z + 4 + (1 - 2 * lax.rem(k, 2)) * ((k + 1) // 2), SIDE)

    def lon_filter(s, group):
        w = weight_rows()
        base = PAD + group * 192 + s * 64
        for b in range(SIDE):
            at = pl.multiple_of(base + 8 * b, 8)
            acc = w[0] * lifted[pl.ds(at, 8), :]
            for tap in range(1, HALF + 1):
                acc = acc + w[tap] * (lifted[pl.ds(at - tap, 8), :] + lifted[pl.ds(at + tap, 8), :])
            along[s, group * SIDE + b] = acc.astype(BF16)

    def lon_first(k, carry):
        lon_filter(0, group_at(k))
        return carry

    lax.fori_loop(0, SIDE, lon_first, 0)
    pl.semaphore_wait(barrier, COL - 1 + MEM - 1)

    for a in FAR_FIRST:
        send_group(0, 0, along, arrived, c, m, lax.rem(z + a, SIDE), a != 0)

    def lon_step(it, carry):
        s, k = it // SIDE, lax.rem(it, SIDE)
        group = group_at(k)
        lon_filter(s, group)
        send_group(0, s, along, arrived, c, m, group, k != SIDE - 1)
        return carry

    lax.fori_loop(SIDE, PARTS * SIDE, lon_step, 0)

    identity = jnp.where(
        lax.broadcasted_iota(jnp.int32, (128, LEV), 0)
        == lax.broadcasted_iota(jnp.int32, (128, LEV), 1),
        1.0, 0.0,
    ).astype(BF16)
    for k in range(3, 7):
        loads[k].wait()
    beta = weights[index[0]]
    for t in range(NLON // 128):
        block = jnp.dot(identity, perturb[0, :, pl.ds(t * 128, 128)], preferred_element_type=F32)
        block = block.T.astype(BF16).reshape(2, 8, 8, 128)
        for half in range(2):
            u = 2 * t + half
            columns[0, u // 3, u % 3] = block[half]
    for k in (4, 3, 5, 2, 6, 1, 7):
        j = lax.rem(m + k, MEM)
        send(2, 0, columns.at[0, j], members.at[0, m], (j, c))
    members[0, m] = columns[0, m]
    first, even, odd = placing_matrices(counts[...].astype(F32))
    place_a[...] = first
    place_b[:, pl.ds(0, 128)] = even
    place_b[:, pl.ds(128, 128)] = odd
    pair_b[pl.ds(0, 64), pl.ds(128, 128)] = jnp.zeros((64, 128), BF16)
    pair_b[pl.ds(64, 64), pl.ds(0, 128)] = jnp.zeros((64, 128), BF16)

    here = z == m
    back_slot = m * SIDE + y
    taps[...] = taps[...] * beta

    def lat_part(s, carry):
        whole(0, s, arrived, COL - 1).wait_recv()
        arrived[s, c] = along[s, c]
        padded[pl.ds(HALF, COL)] = arrived[s].astype(F32)

        def lat_step(k, inner):
            w = weight_rows()
            group = group_at(k)
            for r in range(SIDE):
                at = HALF + group * SIDE + r
                acc = w[0] * padded[at]
                for tap in range(1, HALF + 1):
                    acc = acc + w[tap] * (padded[at - tap] + padded[at + tap])
                smooth[s, group * SIDE + r] = acc.astype(BF16)
            send_group(
                1, s, smooth, back, back_slot, z, group,
                jnp.logical_or(k != SIDE - 1, jnp.logical_not(here)),
            )
            return inner

        lax.fori_loop(0, SIDE, lat_step, 0)
        return carry

    lax.fori_loop(0, PARTS, lat_part, 0)
    whole(2, 0, members, MEM - 1).wait_recv()

    def sum_part(s):
        @pl.when(here)
        def _():
            whole(1, s, back, COL - 1).wait_recv()
            back[s, back_slot] = smooth[s, c]

        @pl.when(jnp.logical_not(here))
        def _():
            whole(1, s, back, COL).wait_recv()

        acc = jnp.zeros((8, 8, 128), F32)
        for k in range(MEM):
            acc = acc + back[s, pl.ds(k * SIDE, SIDE)].astype(F32) * members[0, k, s].astype(F32)
        total[s] = acc.astype(BF16)
        gathered[s, m] = total[s]

    def spread_part(s):
        for k in (4, 3, 5, 2, 6, 1, 7):
            send(3, s, total.at[s], gathered.at[s, m], (lax.rem(m + k, MEM), c))

    def slab_part(kind, place, pair, source, dest, rows):
        source[0] = (
            lax.dot_general(
                place[...], pair[...], (((1,), (1,)), ((), ())), preferred_element_type=F32
            )
            .astype(BF16)
            .reshape(COL, rows, 128)
        )

        for a in FAR_FIRST:
            send_group(kind, 0, source, dest, c, m, lax.rem(z + a, SIDE), a != 0)

    sum_part(0)
    spread_part(0)
    sum_part(1)
    spread_part(1)
    pair_a[pl.ds(0, 64), :] = total[0].reshape(64, 128)
    pair_a[pl.ds(64, 64), :] = total[1].reshape(64, 128)
    slab_part(4, place_a, pair_a, send_a, recv_a, 4)
    sum_part(2)
    last = total[2].reshape(64, 128)
    pair_b[pl.ds(0, 64), pl.ds(0, 128)] = last
    pair_b[pl.ds(64, 64), pl.ds(128, 128)] = last
    slab_part(5, place_b, pair_b, send_b, recv_b, 2)
    spread_part(2)

    def finish(s, carry):
        whole(3, s, gathered, MEM - 1).wait_recv()
        whole(0, s, along, COL - 1).wait_send()

        @pl.when(here)
        def _():
            whole(1, s, smooth, COL - 1).wait_send()

        @pl.when(jnp.logical_not(here))
        def _():
            whole(1, s, smooth, COL).wait_send()

        whole(3, s, gathered, MEM - 1).wait_send()
        return carry

    lax.fori_loop(0, PARTS, finish, 0)
    for t in range(NLON // 128):
        halves = [gathered[u % 3, u // 3].astype(F32).reshape(64, 128) for u in (2 * t, 2 * t + 1)]
        increment_out[:, pl.ds(t * 128, 128)] = jnp.concatenate(halves, axis=0).T[:LEV]
    whole(2, 0, columns, MEM - 1).wait_send()
    whole(4, 0, recv_a, COL - 1).wait_recv()
    recv_a[0, c] = send_a[0, c]
    slab_a_out[...] = recv_a[0]
    whole(5, 0, recv_b, COL - 1).wait_recv()
    recv_b[0, c] = send_b[0, c]
    slab_b_out[...] = recv_b[0]
    whole(4, 0, send_a, COL - 1).wait_send()
    whole(5, 0, send_b, COL - 1).wait_send()


def exchange(controls, perturb, vertical, scales, counts, index, weights):
    block = (8, 128)
    vmem = pl.BlockSpec(memory_space=pltpu.VMEM)
    hbm = pl.BlockSpec(memory_space=pl.ANY)
    return pl.pallas_call(
        exchange_kernel,
        out_shape=(
            jax.ShapeDtypeStruct((LEV, NLON), F32),
            jax.ShapeDtypeStruct((COL, 4, 128), BF16),
            jax.ShapeDtypeStruct((COL, 2, 128), BF16),
        ),
        in_specs=[hbm] * 7,
        out_specs=(vmem, vmem, vmem),
        scratch_shapes=[
            pltpu.VMEM((1, LEV, NLON), BF16),
            pltpu.VMEM((1, LEV, NLON), BF16),
            pltpu.VMEM((LEV, LEV), BF16),
            pltpu.VMEM((1, LEV), F32),
            pltpu.VMEM((1, COL), jnp.int32),
            pltpu.SMEM((1,), jnp.int32),
            pltpu.SMEM((10,), F32),
            pltpu.VMEM((128, LEV), F32),
            pltpu.VMEM((PAD + NLON + PAD, 128), F32),
            pltpu.VMEM((1, 128), F32),
            pltpu.VMEM((PAD, 128), F32),
            pltpu.VMEM((PARTS, COL) + block, BF16),
            pltpu.VMEM((PARTS, COL) + block, BF16),
            pltpu.VMEM((HALF + COL + HALF,) + block, F32),
            pltpu.VMEM((PARTS, COL) + block, BF16),
            pltpu.VMEM((PARTS, COL) + block, BF16),
            pltpu.VMEM((1, MEM, PARTS, 8) + block, BF16),
            pltpu.VMEM((1, MEM, PARTS, 8) + block, BF16),
            pltpu.VMEM((PARTS, 8) + block, BF16),
            pltpu.VMEM((PARTS, MEM, 8) + block, BF16),
            pltpu.VMEM((128, 128), BF16),
            pltpu.VMEM((128, 256), BF16),
            pltpu.VMEM((COL * 4, 128), BF16),
            pltpu.VMEM((COL * 2, 256), BF16),
            pltpu.VMEM((1, COL, 4, 128), BF16),
            pltpu.VMEM((1, COL, 4, 128), BF16),
            pltpu.VMEM((1, COL, 2, 128), BF16),
            pltpu.VMEM((1, COL, 2, 128), BF16),
            pltpu.SemaphoreType.DMA((6, PARTS)),
            pltpu.SemaphoreType.DMA((6, PARTS)),
            pltpu.SemaphoreType.DMA((7,)),
        ],
        compiler_params=pltpu.CompilerParams(
            collective_id=0, has_side_effects=True, vmem_limit_bytes=32 * 1024 * 1024
        ),
        name="exchange",
    )(
        *(
            pltpu.with_memory_space_constraint(x, pltpu.HBM)
            for x in (controls, perturb, vertical, scales, counts)
        ),
        index, pltpu.with_memory_space_constraint(weights, pltpu.HBM),
    )


def arrange_kernel(ready, slab_a, slab_b, increment, slab_increment, rows_a, rows_b, slots, sems):
    whole = pltpu.make_async_copy(ready, increment, sems.at[0])
    whole.start()
    rows_a[...] = slab_a[...].astype(F32).reshape(COL * 4, 128)
    rows_b[...] = slab_b[...].astype(F32).reshape(COL * 2, 128)
    for q in range(4):
        slots[q, :, pl.ds(0, 128)] = rows_a[pl.ds(q, COL, stride=4), :]
    for r in range(2):
        both = rows_b[pl.ds(r, COL, stride=2), :]
        slots[2 * r, :, pl.ds(128, 64)] = both[:, :64]
        slots[2 * r + 1, :, pl.ds(128, 64)] = both[:, 64:]
    owned = pltpu.make_async_copy(slots, slab_increment, sems.at[1])
    owned.start()
    whole.wait()
    owned.wait()


def arrange(ready, slab_a, slab_b):
    vmem = pl.BlockSpec(memory_space=pltpu.VMEM)
    hbm = pl.BlockSpec(memory_space=pl.ANY)
    return pl.pallas_call(
        arrange_kernel,
        out_shape=(
            jax.ShapeDtypeStruct((LEV, NLON), F32),
            jax.ShapeDtypeStruct((4, COL, 192), F32),
        ),
        in_specs=[vmem, vmem, vmem],
        out_specs=(hbm, hbm),
        scratch_shapes=[
            pltpu.VMEM((COL * 4, 128), F32),
            pltpu.VMEM((COL * 2, 128), F32),
            pltpu.VMEM((4, COL, 192), F32),
            pltpu.SemaphoreType.DMA((2,)),
        ],
        compiler_params=pltpu.CompilerParams(vmem_limit_bytes=16 * 1024 * 1024),
        name="arrange",
    )(ready, slab_a, slab_b)


def on_device(
    controls, perturbations, vertical_filter, scales, level_counts, weight_index, member_weights
):
    outs = exchange(
        controls, perturbations, vertical_filter, scales[None, :],
        level_counts[None, :], weight_index, member_weights,
    )
    return arrange(*outs)


def solution(mesh):
    return jax.shard_map(
        on_device,
        mesh=mesh,
        in_specs=(P("mem", None, "col"), P("mem", None, "col"), P(), P(), P(), P("mem"), P()),
        out_specs=(P(None, "col"), P("col", None, "mem")),
        check_vma=False,
    )
```

```python
import jax
import jax.numpy as jnp
from jax import lax
from jax.experimental import pallas as pl
from jax.experimental.pallas import tpu as pltpu
from jax.sharding import PartitionSpec as P

LEV = 127
NLON = 1536
HALF = 24
MEM = 8
COL = 64
SIDE = 8
PARTS = 3
PAD = 32
MESH = pl.DeviceIdType.MESH
FAR_FIRST = (4, 3, 5, 2, 6, 1, 7, 0)
F32 = jnp.float32
BF16 = jnp.bfloat16


def taps_rows(width):
    rows = lax.broadcasted_iota(jnp.int32, (PAD, 128), 0).astype(F32)
    raw = jnp.exp(-(rows * rows) / (2.0 * width * width))
    squares = jnp.where(rows <= HALF, jnp.exp(-(rows * rows) / (width * width)), 0.0)
    normal = jnp.sqrt(2.0 * jnp.sum(squares, axis=0, keepdims=True) - 1.0)
    return (raw / normal).astype(BF16).astype(F32)


def placing_matrices(counts):
    def starts_counts(tile, rows):
        lane = lax.broadcasted_iota(jnp.int32, (rows, COL), 1)
        start = jnp.sum(jnp.where(lane < tile, counts, 0.0), axis=1, keepdims=True)
        count = jnp.sum(jnp.where(lane == tile, counts, 0.0), axis=1, keepdims=True)
        return start, count

    row = lax.broadcasted_iota(jnp.int32, (COL * 4, 1), 0)
    start, count = starts_counts(row // 4, COL * 4)
    slot = lax.rem(row, 4).astype(F32)
    target = jnp.where(slot < count, start + slot, -1.0)
    lane = lax.broadcasted_iota(jnp.int32, (COL * 4, 128), 1).astype(F32)
    first = jnp.where(lane == target, 1.0, 0.0).astype(BF16)
    row = lax.broadcasted_iota(jnp.int32, (COL * 2, 1), 0)
    start, count = starts_counts(row // 2, COL * 2)
    lane = lax.broadcasted_iota(jnp.int32, (COL * 2, 128), 1).astype(F32)
    both = []
    for odd in range(2):
        slot = (2 * lax.rem(row, 2) + odd).astype(F32)
        target = jnp.where(slot < count, start + slot, -1.0)
        both.append(jnp.where(lane == target, 1.0, 0.0).astype(BF16))
    return first, both[0], both[1]


def exchange_kernel(
    controls_hbm, perturb_hbm, vertical_hbm, scales_hbm, counts_hbm, index_hbm, weights_hbm,
    increment_out, slab_a_out, slab_b_out,
    controls, perturb, vertical, scales, counts, index, weights,
    matrix_rows, lifted, width_row, taps, along, arrived, padded, smooth, back, columns, members,
    total, gathered, pair_a, pair_b, place_a, place_b,
    send_a, recv_a, send_b, recv_b,
    send_sems, recv_sems, load_sems,
):
    m = lax.axis_index("mem")
    c = lax.axis_index("col")
    z, y = c // SIDE, lax.rem(c, SIDE)

    loads = [
        pltpu.make_async_copy(src, dst, load_sems.at[k])
        for k, (src, dst) in enumerate(
            (
                (vertical_hbm, vertical), (controls_hbm, controls), (scales_hbm, scales),
                (counts_hbm, counts), (index_hbm, index), (weights_hbm, weights),
                (perturb_hbm, perturb),
            )
        )
    ]
    for load in loads:
        load.start()

    barrier = pltpu.get_barrier_semaphore()
    for a in FAR_FIRST:
        zz = lax.rem(z + a, SIDE) * SIDE
        for b in FAR_FIRST:
            if a or b:
                pl.semaphore_signal(
                    barrier, inc=1, device_id=(m, zz + lax.rem(y + b, SIDE)), device_id_type=MESH
                )
    for k in range(1, MEM):
        pl.semaphore_signal(barrier, inc=1, device_id=(lax.rem(m + k, MEM), c), device_id_type=MESH)

    matrix_rows[pl.ds(LEV, 1), :] = jnp.zeros((1, LEV), F32)
    loads[0].wait()
    matrix_rows[pl.ds(0, LEV), :] = vertical[...].astype(F32)
    filter_rows = matrix_rows[...].astype(BF16)
    loads[1].wait()
    for t in range(NLON // 128):
        block = jnp.dot(
            filter_rows, controls[0, :, pl.ds(t * 128, 128)], preferred_element_type=F32
        )
        lifted[pl.ds(PAD + t * 128, 128), :] = block.astype(BF16).astype(F32).T
    lifted[pl.ds(0, PAD), :] = lifted[pl.ds(NLON, PAD), :]
    lifted[pl.ds(PAD + NLON, PAD), :] = lifted[pl.ds(PAD, PAD), :]

    width_row[...] = jnp.full((1, 128), 16.0, F32)
    loads[2].wait()
    width_row[:, :LEV] = scales[...]
    taps[...] = taps_rows(width_row[...])
    padded[pl.ds(0, HALF)] = jnp.zeros((HALF, 8, 128), F32)
    padded[pl.ds(HALF + COL, HALF)] = jnp.zeros((HALF, 8, 128), F32)

    def weight_rows():
        return [jnp.broadcast_to(taps[k : k + 1, :], (8, 128)) for k in range(HALF + 1)]

    def send(kind, s, src, dst, device):
        pltpu.make_async_remote_copy(
            src_ref=src, dst_ref=dst,
            send_sem=send_sems.at[kind, s], recv_sem=recv_sems.at[kind, s],
            device_id=device, device_id_type=MESH,
        ).start()

    def whole(kind, s, ref, count):
        part = ref.at[s, pl.ds(0, count)]
        return pltpu.make_async_remote_copy(
            src_ref=part, dst_ref=part,
            send_sem=send_sems.at[kind, s], recv_sem=recv_sems.at[kind, s],
            device_id=(m, c), device_id_type=MESH,
        )

    def send_group(kind, s, source, dest, slot, member, group, away):
        for b in FAR_FIRST:
            row = group * SIDE + lax.rem(y + b, SIDE)
            if b or away is True:
                send(kind, s, source.at[s, row], dest.at[s, slot], (member, row))
            elif away is not False:
                @pl.when(away)
                def _():
                    send(kind, s, source.at[s, row], dest.at[s, slot], (member, row))

    def group_at(k):
        return lax.rem(z + 4 + (1 - 2 * lax.rem(k, 2)) * ((k + 1) // 2), SIDE)

    def lon_filter(s, group):
        w = weight_rows()
        base = PAD + group * 192 + s * 64
        at = pl.multiple_of(base, 8)
        for b in range(SIDE):
            mid = at + 8 * b
            acc = w[0] * lifted[pl.ds(mid, 8), :]
            for tap in range(1, HALF + 1):
                acc = acc + w[tap] * (
                    lifted[pl.ds(mid - tap, 8), :] + lifted[pl.ds(mid + tap, 8), :]
                )
            along[s, group * SIDE + b] = acc.astype(BF16)

    def lon_first(k, carry):
        lon_filter(0, group_at(k))
        return carry

    lax.fori_loop(0, SIDE, lon_first, 0)
    pl.semaphore_wait(barrier, COL - 1 + MEM - 1)

    for a in FAR_FIRST:
        send_group(0, 0, along, arrived, c, m, lax.rem(z + a, SIDE), a != 0)

    def lon_step(it, carry):
        s, k = it // SIDE, lax.rem(it, SIDE)
        group = group_at(k)
        lon_filter(s, group)
        send_group(0, s, along, arrived, c, m, group, k != SIDE - 1)
        return carry

    lax.fori_loop(SIDE, PARTS * SIDE, lon_step, 0)

    identity = jnp.where(
        lax.broadcasted_iota(jnp.int32, (128, LEV), 0)
        == lax.broadcasted_iota(jnp.int32, (128, LEV), 1),
        1.0, 0.0,
    ).astype(BF16)
    for k in range(3, 7):
        loads[k].wait()
    beta = weights[index[0]]
    for t in range(NLON // 128):
        block = jnp.dot(identity, perturb[0, :, pl.ds(t * 128, 128)], preferred_element_type=F32)
        block = block.T.astype(BF16).reshape(2, 8, 8, 128)
        for half in range(2):
            u = 2 * t + half
            columns[0, u // 3, u % 3] = block[half]
    for k in (4, 3, 5, 2, 6, 1, 7):
        j = lax.rem(m + k, MEM)
        send(2, 0, columns.at[0, j], members.at[0, m], (j, c))
    members[0, m] = columns[0, m]
    first, even, odd = placing_matrices(counts[...].astype(F32))
    place_a[...] = first
    place_b[:, pl.ds(0, 128)] = even
    place_b[:, pl.ds(128, 128)] = odd
    pair_b[pl.ds(0, 64), pl.ds(128, 128)] = jnp.zeros((64, 128), BF16)
    pair_b[pl.ds(64, 64), pl.ds(0, 128)] = jnp.zeros((64, 128), BF16)

    here = z == m
    back_slot = m * SIDE + y
    taps[...] = taps[...] * beta

    def lat_part(s, carry):
        whole(0, s, arrived, COL - 1).wait_recv()
        arrived[s, c] = along[s, c]
        padded[pl.ds(HALF, COL)] = arrived[s].astype(F32)

        def lat_step(k, inner):
            w = weight_rows()
            group = group_at(k)
            for r in range(0, SIDE, 4):
                at = HALF + group * SIDE + r
                low = [padded[at + i] for i in range(4)]
                high = low
                acc = [w[0] * value for value in low]
                for tap in range(1, HALF + 1):
                    low = [padded[at - tap]] + low[:3]
                    high = high[1:] + [padded[at + 3 + tap]]
                    acc = [a + w[tap] * (p + q) for a, p, q in zip(acc, low, high)]
                for i in range(4):
                    smooth[s, group * SIDE + r + i] = acc[i].astype(BF16)
            send_group(
                1, s, smooth, back, back_slot, z, group,
                jnp.logical_or(k != SIDE - 1, jnp.logical_not(here)),
            )
            return inner

        lax.fori_loop(0, SIDE, lat_step, 0)
        return carry

    lax.fori_loop(0, PARTS, lat_part, 0)
    whole(2, 0, members, MEM - 1).wait_recv()

    def sum_part(s):
        @pl.when(here)
        def _():
            whole(1, s, back, COL - 1).wait_recv()
            back[s, back_slot] = smooth[s, c]

        @pl.when(jnp.logical_not(here))
        def _():
            whole(1, s, back, COL).wait_recv()

        acc = jnp.zeros((8, 8, 128), F32)
        for k in range(MEM):
            acc = acc + back[s, pl.ds(k * SIDE, SIDE)].astype(F32) * members[0, k, s].astype(F32)
        total[s] = acc.astype(BF16)
        gathered[s, m] = total[s]

    def spread_part(s):
        for k in (4, 3, 5, 2, 6, 1, 7):
            send(3, s, total.at[s], gathered.at[s, m], (lax.rem(m + k, MEM), c))

    def slab_part(kind, place, pair, source, dest, rows):
        source[0] = (
            lax.dot_general(
                place[...], pair[...], (((1,), (1,)), ((), ())), preferred_element_type=F32
            )
            .astype(BF16)
            .reshape(COL, rows, 128)
        )

        for a in FAR_FIRST:
            send_group(kind, 0, source, dest, c, m, lax.rem(z + a, SIDE), a != 0)

    sum_part(0)
    spread_part(0)
    sum_part(1)
    spread_part(1)
    pair_a[pl.ds(0, 64), :] = total[0].reshape(64, 128)
    pair_a[pl.ds(64, 64), :] = total[1].reshape(64, 128)
    slab_part(4, place_a, pair_a, send_a, recv_a, 4)
    sum_part(2)
    last = total[2].reshape(64, 128)
    pair_b[pl.ds(0, 64), pl.ds(0, 128)] = last
    pair_b[pl.ds(64, 64), pl.ds(128, 128)] = last
    slab_part(5, place_b, pair_b, send_b, recv_b, 2)
    spread_part(2)

    def finish(s, carry):
        whole(3, s, gathered, MEM - 1).wait_recv()
        whole(0, s, along, COL - 1).wait_send()

        @pl.when(here)
        def _():
            whole(1, s, smooth, COL - 1).wait_send()

        @pl.when(jnp.logical_not(here))
        def _():
            whole(1, s, smooth, COL).wait_send()

        whole(3, s, gathered, MEM - 1).wait_send()
        return carry

    lax.fori_loop(0, PARTS, finish, 0)
    for t in range(NLON // 128):
        halves = [gathered[u % 3, u // 3].astype(F32).reshape(64, 128) for u in (2 * t, 2 * t + 1)]
        increment_out[:, pl.ds(t * 128, 128)] = jnp.concatenate(halves, axis=0).T[:LEV]
    whole(2, 0, columns, MEM - 1).wait_send()
    whole(4, 0, recv_a, COL - 1).wait_recv()
    recv_a[0, c] = send_a[0, c]
    slab_a_out[...] = recv_a[0]
    whole(5, 0, recv_b, COL - 1).wait_recv()
    recv_b[0, c] = send_b[0, c]
    slab_b_out[...] = recv_b[0]
    whole(4, 0, send_a, COL - 1).wait_send()
    whole(5, 0, send_b, COL - 1).wait_send()


def exchange(controls, perturb, vertical, scales, counts, index, weights):
    block = (8, 128)
    vmem = pl.BlockSpec(memory_space=pltpu.VMEM)
    hbm = pl.BlockSpec(memory_space=pl.ANY)
    return pl.pallas_call(
        exchange_kernel,
        out_shape=(
            jax.ShapeDtypeStruct((LEV, NLON), F32),
            jax.ShapeDtypeStruct((COL, 4, 128), BF16),
            jax.ShapeDtypeStruct((COL, 2, 128), BF16),
        ),
        in_specs=[hbm] * 7,
        out_specs=(vmem, vmem, vmem),
        scratch_shapes=[
            pltpu.VMEM((1, LEV, NLON), BF16),
            pltpu.VMEM((1, LEV, NLON), BF16),
            pltpu.VMEM((LEV, LEV), BF16),
            pltpu.VMEM((1, LEV), F32),
            pltpu.VMEM((1, COL), jnp.int32),
            pltpu.SMEM((1,), jnp.int32),
            pltpu.SMEM((10,), F32),
            pltpu.VMEM((128, LEV), F32),
            pltpu.VMEM((PAD + NLON + PAD, 128), F32),
            pltpu.VMEM((1, 128), F32),
            pltpu.VMEM((PAD, 128), F32),
            pltpu.VMEM((PARTS, COL) + block, BF16),
            pltpu.VMEM((PARTS, COL) + block, BF16),
            pltpu.VMEM((HALF + COL + HALF,) + block, F32),
            pltpu.VMEM((PARTS, COL) + block, BF16),
            pltpu.VMEM((PARTS, COL) + block, BF16),
            pltpu.VMEM((1, MEM, PARTS, 8) + block, BF16),
            pltpu.VMEM((1, MEM, PARTS, 8) + block, BF16),
            pltpu.VMEM((PARTS, 8) + block, BF16),
            pltpu.VMEM((PARTS, MEM, 8) + block, BF16),
            pltpu.VMEM((128, 128), BF16),
            pltpu.VMEM((128, 256), BF16),
            pltpu.VMEM((COL * 4, 128), BF16),
            pltpu.VMEM((COL * 2, 256), BF16),
            pltpu.VMEM((1, COL, 4, 128), BF16),
            pltpu.VMEM((1, COL, 4, 128), BF16),
            pltpu.VMEM((1, COL, 2, 128), BF16),
            pltpu.VMEM((1, COL, 2, 128), BF16),
            pltpu.SemaphoreType.DMA((6, PARTS)),
            pltpu.SemaphoreType.DMA((6, PARTS)),
            pltpu.SemaphoreType.DMA((7,)),
        ],
        compiler_params=pltpu.CompilerParams(
            collective_id=0, has_side_effects=True, vmem_limit_bytes=32 * 1024 * 1024
        ),
        name="exchange",
    )(
        *(
            pltpu.with_memory_space_constraint(x, pltpu.HBM)
            for x in (controls, perturb, vertical, scales, counts)
        ),
        index, pltpu.with_memory_space_constraint(weights, pltpu.HBM),
    )


def arrange_kernel(ready, slab_a, slab_b, increment, slab_increment, rows_a, rows_b, slots, sems):
    whole = pltpu.make_async_copy(ready, increment, sems.at[0])
    whole.start()
    rows_a[...] = slab_a[...].astype(F32).reshape(COL * 4, 128)
    rows_b[...] = slab_b[...].astype(F32).reshape(COL * 2, 128)
    for q in range(4):
        slots[q, :, pl.ds(0, 128)] = rows_a[pl.ds(q, COL, stride=4), :]
    for r in range(2):
        both = rows_b[pl.ds(r, COL, stride=2), :]
        slots[2 * r, :, pl.ds(128, 64)] = both[:, :64]
        slots[2 * r + 1, :, pl.ds(128, 64)] = both[:, 64:]
    owned = pltpu.make_async_copy(slots, slab_increment, sems.at[1])
    owned.start()
    whole.wait()
    owned.wait()


def arrange(ready, slab_a, slab_b):
    vmem = pl.BlockSpec(memory_space=pltpu.VMEM)
    hbm = pl.BlockSpec(memory_space=pl.ANY)
    return pl.pallas_call(
        arrange_kernel,
        out_shape=(
            jax.ShapeDtypeStruct((LEV, NLON), F32),
            jax.ShapeDtypeStruct((4, COL, 192), F32),
        ),
        in_specs=[vmem, vmem, vmem],
        out_specs=(hbm, hbm),
        scratch_shapes=[
            pltpu.VMEM((COL * 4, 128), F32),
            pltpu.VMEM((COL * 2, 128), F32),
            pltpu.VMEM((4, COL, 192), F32),
            pltpu.SemaphoreType.DMA((2,)),
        ],
        compiler_params=pltpu.CompilerParams(vmem_limit_bytes=16 * 1024 * 1024),
        name="arrange",
    )(ready, slab_a, slab_b)


def on_device(
    controls, perturbations, vertical_filter, scales, level_counts, weight_index, member_weights
):
    outs = exchange(
        controls, perturbations, vertical_filter, scales[None, :],
        level_counts[None, :], weight_index, member_weights,
    )
    return arrange(*outs)


def solution(mesh):
    return jax.shard_map(
        on_device,
        mesh=mesh,
        in_specs=(P("mem", None, "col"), P("mem", None, "col"), P(), P(), P(), P("mem"), P()),
        out_specs=(P(None, "col"), P("col", None, "mem")),
        check_vma=False,
    )
```
